32 devices in a mesh: group: 2 (over y), tensor: 8 (over z, x), seq: 2 (over core).
Axes of the slice: x: 2, y: 2, z: 4, core: 2. Of those that a mesh axis runs over, the one named last changes fastest.
Arguments:
- tokens: bfloat16 [512, 8192], P(('group', 'seq'), 'tensor'), parts along dimension 0, may hold values from -6 to 6
- gate_tiles: bfloat16 [768, 128, 128], P(('tensor', 'seq')), may hold values from -0.09375 to 0.09375
- up_tiles: bfloat16 [768, 128, 128], P(('tensor', 'seq')), may hold values from -0.09375 to 0.09375
- down_tiles: bfloat16 [768, 128, 128], P(('tensor', 'seq')), may hold values from -0.1875 to 0.1875
- in_mask: int32 [16, 64], P('tensor'), may hold values from 0 to 1, as said below
- out_mask: int32 [16, 64], P('tensor'), may hold values from 0 to 1, as said below
- owner_core: int32 [512], P('group'), parts along dimension 0, may hold values from 0 to 1, as said below
Outputs:
- owned: bfloat16 [768, 8192], P(('group', 'seq'), 'tensor'), parts along dimension 0
The draws below stay inside these ranges and needn't reach their ends.
There are 2 independent parts, one for each index of `group`. The reference program is written for one: setup_inputs(seed, part) draws one part's arguments, and reference() takes and returns one part's arrays. A program takes and returns all parts, laid end to end along the dimension named above; an argument that names none is the same for every part. Nothing has to cross between parts.
Inputs may be any that keep to these rules, and one draw needn't show every extreme that they name: `in_mask`: in each group of 2 consecutive rows (the hidden blocks of one tensor index) at most 96 entries are 1, and some group holds exactly 96. `out_mask`: in each group of 2 consecutive rows at most 96 entries are 1, and some group holds exactly 96. `owner_core`: one core owns exactly 192 tokens, forming one run of the cyclic token order; the other core owns the rest.
All inputs are finite; a program needn't handle non-finite values.
Results may differ from the reference program's by a relative error of at most 0.0049.
Values may be sent and summed in bfloat16 or wider, within the bound.
A program may use at most 128 MiB of HBM per device.

```python
import jax
import jax.numpy as jnp
from jax import lax

BLOCK = 128
D = 8192
HB = 2
CAP = 96
OWN_CAP = 192
TOKENS = 256
DB = 64
FB = 16
FF = 2048
N_TENSOR = 8
N_SEQ = 2


def block_mask(key):
    shard_count = FB // HB
    entries = HB * DB
    key_count, key_top, key_score = jax.random.split(key, 3)
    counts = jax.random.randint(key_count, (shard_count,), CAP // 3, CAP + 1)
    busiest = jax.random.randint(key_top, (), 0, shard_count)
    counts = jnp.where(jnp.arange(shard_count) == busiest, CAP, counts)
    scores = jax.random.randint(key_score, (shard_count, entries), 0, 1 << 20) * entries + jnp.arange(entries)[None, :]
    ordering = jnp.argsort(scores, axis=1)
    rank_of = jnp.argsort(ordering, axis=1)
    return (rank_of < counts[:, None]).astype(jnp.int32).reshape(FB, DB)


def draw_in_mask(key, part):
    key = jax.random.fold_in(key, 11)
    return block_mask(key)


def draw_out_mask(key, part):
    key = jax.random.fold_in(key, 23)
    return block_mask(key)


def draw_owner_core(key, part):
    key = jax.random.fold_in(key, 37)
    key_start, key_core = jax.random.split(key)
    run_start = jax.random.randint(key_start, (), 0, TOKENS)
    big_core = jax.random.randint(key_core, (), 0, 2)
    positions = jnp.arange(TOKENS, dtype=jnp.int32)
    inside = jnp.mod(positions - run_start, TOKENS) < OWN_CAP
    return jnp.where(inside, big_core, 1 - big_core).astype(jnp.int32)


def levels(key, dims, shards, least, high):
    factor_of, own = 1.0, jax.random.fold_in(key, 6)
    for position, parts in shards:
        draws = jnp.exp(jax.random.uniform(jax.random.fold_in(own, position), (parts,), jnp.float32, least / len(shards), high / len(shards)))
        factor_of = factor_of * jnp.repeat(draws, dims[position] // parts).reshape([-1 if axis == position else 1 for axis in range(len(dims))])
    return factor_of


def bell_draw(stream_key, shape, width, most, cuts=(), kind=jnp.bfloat16):
    drawn = width * jax.random.normal(stream_key, shape, jnp.float32)
    if cuts:
        drawn = drawn * levels(stream_key, shape, cuts, -0.22, 0.18)
    return jnp.clip(drawn, -most, most).astype(kind)


def setup_inputs(seed: int = 0, part: int = 0) -> dict:
    arg_keys = jax.random.split(jax.random.key(seed), 8)
    part_keys = jax.random.split(jax.random.fold_in(arg_keys[7], part), 8)
    tokens = bell_draw(part_keys[0], (TOKENS, D), 1.0, 6.0, ((0, 2), (1, 8)))
    gate_tiles = bell_draw(arg_keys[1], (CAP * N_TENSOR, BLOCK, BLOCK), (D // 2) ** -0.5, 0.09375, ((0, 16),))
    up_tiles = bell_draw(arg_keys[2], (CAP * N_TENSOR, BLOCK, BLOCK), (D // 2) ** -0.5, 0.09375, ((0, 16),))
    down_tiles = bell_draw(arg_keys[3], (CAP * N_TENSOR, BLOCK, BLOCK), (FF // 2) ** -0.5, 0.1875, ((0, 16),))
    in_mask = draw_in_mask(jax.random.fold_in(arg_keys[7], 71), part)
    out_mask = draw_out_mask(jax.random.fold_in(arg_keys[7], 71), part)
    owner_core = draw_owner_core(jax.random.fold_in(jax.random.fold_in(arg_keys[7], part), 71), part)
    return dict(tokens=tokens, gate_tiles=gate_tiles, up_tiles=up_tiles, down_tiles=down_tiles, in_mask=in_mask, out_mask=out_mask, owner_core=owner_core)


def slot_table(mask_rows, capacity):
    hidden_blocks, width_blocks = mask_rows.shape
    flat_mask = mask_rows.reshape(-1).astype(jnp.int32)
    rank_of = (jnp.cumsum(flat_mask) - 1).astype(jnp.int32)
    entries = jnp.arange(hidden_blocks * width_blocks, dtype=jnp.int32)
    slot_ids = jnp.arange(capacity, dtype=jnp.int32)
    matched = ((flat_mask[:, None] == 1) & (rank_of[:, None] == slot_ids[None, :])).astype(jnp.int32)
    live_flag = jnp.sum(matched, axis=0).astype(jnp.int32)
    width_index = jnp.sum(matched * (entries % width_blocks)[:, None], axis=0).astype(jnp.int32)
    hidden_index = jnp.sum(matched * (entries // width_blocks)[:, None], axis=0).astype(jnp.int32)
    return width_index, hidden_index, live_flag


def dense_input(tiles, mask_rows):
    hidden_blocks, width_blocks = mask_rows.shape
    block_size = tiles.shape[1]
    width_index, hidden_index, live_flag = slot_table(mask_rows, tiles.shape[0])
    weighted = tiles * live_flag[:, None, None].astype(tiles.dtype)
    grid_tiles = jnp.zeros((width_blocks, hidden_blocks, block_size, block_size), tiles.dtype)
    grid_tiles = grid_tiles.at[width_index, hidden_index].add(weighted)
    return grid_tiles.transpose(0, 2, 1, 3).reshape(width_blocks * block_size, hidden_blocks * block_size)


def dense_output(tiles, mask_rows):
    hidden_blocks, width_blocks = mask_rows.shape
    block_size = tiles.shape[1]
    width_index, hidden_index, live_flag = slot_table(mask_rows, tiles.shape[0])
    weighted = tiles * live_flag[:, None, None].astype(tiles.dtype)
    grid_tiles = jnp.zeros((hidden_blocks, width_blocks, block_size, block_size), tiles.dtype)
    grid_tiles = grid_tiles.at[hidden_index, width_index].add(weighted)
    return grid_tiles.transpose(0, 2, 1, 3).reshape(hidden_blocks * block_size, width_blocks * block_size)


def reference(tokens, gate_tiles, up_tiles, down_tiles, in_mask, out_mask, owner_core):
    shard_count = in_mask.shape[0] // HB

    def one_shard(running, shard_index):
        tile_start = (shard_index * CAP).astype(jnp.int32)
        mask_start = (shard_index * HB).astype(jnp.int32)
        mask_in = lax.dynamic_slice_in_dim(in_mask, mask_start, HB, 0)
        mask_out = lax.dynamic_slice_in_dim(out_mask, mask_start, HB, 0)
        w_gate = dense_input(lax.dynamic_slice_in_dim(gate_tiles, tile_start, CAP, 0), mask_in)
        w_up = dense_input(lax.dynamic_slice_in_dim(up_tiles, tile_start, CAP, 0), mask_in)
        w_down = dense_output(lax.dynamic_slice_in_dim(down_tiles, tile_start, CAP, 0), mask_out)
        gate_sum = jnp.dot(tokens, w_gate, preferred_element_type=jnp.float32)
        up_sum = jnp.dot(tokens, w_up, preferred_element_type=jnp.float32)
        hidden = (jax.nn.silu(gate_sum) * up_sum).astype(jnp.bfloat16)
        return running + jnp.dot(hidden, w_down, preferred_element_type=jnp.float32), None

    total, _ = lax.scan(one_shard, jnp.zeros((TOKENS, D), jnp.float32), jnp.arange(shard_count, dtype=jnp.int32))
    mixed_rows = total.astype(jnp.bfloat16)
    pieces = []
    out_ids = jnp.arange(OWN_CAP, dtype=jnp.int32)
    for core_index in range(N_SEQ):
        owned_flag = (owner_core == core_index).astype(jnp.int32)
        order_in = (jnp.cumsum(owned_flag) - 1).astype(jnp.int32)
        placing = ((owned_flag[None, :] == 1) & (order_in[None, :] == out_ids[:, None])).astype(jnp.bfloat16)
        pieces.append(jnp.dot(placing, mixed_rows, preferred_element_type=jnp.float32).astype(jnp.bfloat16))
    return jnp.concatenate(pieces, axis=0)
```

```python
import functools

import jax
import jax.numpy as jnp
from jax import lax
from jax.experimental import pallas as pl
from jax.experimental.pallas import tpu as pltpu
from jax.sharding import PartitionSpec as P

CAP = 96
OWN_CAP = 192
MESH = pl.DeviceIdType.MESH


def grid_of(n_tensor):
    n_x = 1 << ((n_tensor.bit_length() - 1) // 2)
    return n_tensor // n_x, n_x


def less(a, b, n):
    return lax.div(b - a + n, n + 1)


def by_distance(z, j, n_z):
    flip = less(n_z - 1 - z, z, n_z)
    near = z + flip * (n_z - 1 - 2 * z)
    k = lax.div(j + 1, 2)
    both = z + k * (1 - 2 * lax.rem(j, 2))
    one = j + flip * (n_z - 1 - 2 * j)
    far = less(2 * near, j, 2 * n_z)
    return both + far * (one - both)


def kernel(
    n_z,
    tokens,
    gate_tiles,
    up_tiles,
    down_tiles,
    in_mask,
    out_mask,
    owner,
    out,
    feats,
    gates,
    ups,
    downs,
    slots_in,
    slots_out,
    acc,
    hidden,
    x_out,
    x_in,
    z_out,
    z_in,
    mixed,
    tile_local,
    tile_send,
    tile_recv,
    own_copy,
    feat_recv,
    own_send,
    feat_z_send,
    feat_x_send,
    sum_x_send,
    sum_x_recv,
    sum_z_send,
    sum_z_recv,
    mix_sems,
):
    t = lax.axis_index("tensor")
    s = lax.axis_index("seq")
    z, x = lax.div(t, 2), lax.rem(t, 2)
    rows, width = tokens.shape
    half, block = gate_tiles.shape[0], gate_tiles.shape[1]
    cap = 2 * half
    n_blocks = in_mask.shape[1]
    per_part = width // block
    pair = 2 * block

    def dev(tt, ss=None):
        return {"tensor": tt, "seq": s if ss is None else ss}

    def at(zz, xx):
        return zz * 2 + xx

    x_peer = at(z, 1 - x)
    core_peer = dev(t, 1 - s)

    barrier = pltpu.get_barrier_semaphore()

    def greet(device):
        pl.semaphore_signal(barrier, inc=1, device_id=device, device_id_type=MESH)

    greet(core_peer)
    greet(dev(x_peer))

    @pl.when(z > 0)
    def _():
        greet(dev(at(z - 1, x)))

    @pl.when(z < n_z - 1)
    def _():
        greet(dev(at(z + 1, x)))

    for dst in (gates, ups, downs):
        dst[cap] = jnp.zeros((block, block), dst.dtype)
    acc[...] = jnp.zeros_like(acc)

    local = []
    for i, (src, dst) in enumerate(((gate_tiles, gates), (up_tiles, ups), (down_tiles, downs))):
        copy = pltpu.make_async_copy(src, dst.at[pl.ds(s * half, half)], tile_local.at[i])
        local.append(copy)
    own = pltpu.make_async_copy(tokens, feats.at[t], own_copy)
    own.start()
    for copy in local:
        copy.start()

    @pl.when((z > 0) & (z < n_z - 1))
    def _():
        pl.semaphore_wait(barrier, 4)

    @pl.when((z == 0) | (z == n_z - 1))
    def _():
        pl.semaphore_wait(barrier, 3)

    def send(src, dst, send_sem, recv_sem, device):
        return pltpu.make_async_remote_copy(
            src_ref=src,
            dst_ref=dst,
            send_sem=send_sem,
            recv_sem=recv_sem,
            device_id=device,
            device_id_type=MESH,
        )

    def own_to(zz, k):
        return send(tokens, feats.at[t], own_send.at[k], feat_recv.at[t], dev(at(zz, x)))

    own_x = send(tokens, feats.at[t], own_send.at[2], feat_recv.at[t], dev(x_peer))
    own_x.start()

    @pl.when(z > 0)
    def _():
        own_to(z - 1, 0).start()

    @pl.when(z < n_z - 1)
    def _():
        own_to(z + 1, 1).start()

    remote = []
    for i, (src, dst) in enumerate(((gate_tiles, gates), (up_tiles, ups), (down_tiles, downs))):
        copy = send(
            src, dst.at[pl.ds(s * half, half)], tile_send.at[i], tile_recv.at[i], core_peer
        )
        copy.start()
        remote.append(copy)

    for mask, table in ((in_mask, slots_in), (out_mask, slots_out)):
        for c in range(2):

            def fill(b, count, c=c, mask=mask, table=table):
                bit = mask[c, b]
                table[c, b] = jnp.where(bit == 1, count, cap)
                return count + bit

            total = lax.fori_loop(0, n_blocks, fill, jnp.int32(0) if c == 0 else total)

    for i in range(2):
        local[i].wait()
        remote[i].wait_recv()
    own.wait()

    def project(part):
        def step(i, carry):
            b = part * per_part + 2 * i
            a = feats[part, :, pl.ds(pl.multiple_of(i * pair, pair), pair)]
            for m, tiles in enumerate((gates, ups)):
                cols = [
                    jnp.concatenate(
                        [tiles[slots_in[c, b]], tiles[slots_in[c, b + 1]]], axis=0
                    )
                    for c in range(2)
                ]
                w = jnp.concatenate(cols, axis=1)
                acc[m] += jnp.dot(a, w, preferred_element_type=jnp.float32)
            return carry

        lax.fori_loop(0, per_part // 2, step, 0)

    def arrived(part):
        send(
            feats.at[part], feats.at[part], own_send.at[2], feat_recv.at[part], dev(x_peer)
        ).wait_recv()

    def forward_x(src):
        part = at(src, x)
        return send(
            feats.at[part], feats.at[part], feat_x_send.at[src], feat_recv.at[part], dev(x_peer)
        )

    def forward_z(src):
        part = at(src, x)
        to = z - 1 + 2 * less(src, z, n_z)
        return send(
            feats.at[part], feats.at[part], feat_z_send.at[src], feat_recv.at[part],
            dev(at(to, x)),
        )

    def goes_on(src):
        return ((src < z) & (z < n_z - 1)) | ((src > z) & (z > 0))

    project(t)

    def gather_step(j, carry):
        src = by_distance(z, j, n_z)
        arrived(at(src, x))

        @pl.when(goes_on(src))
        def _():
            forward_z(src).start()

        forward_x(src).start()
        before = at(by_distance(z, j - 1, n_z), 1 - x)
        project(at(src, x))
        arrived(before)
        project(before)
        return carry

    lax.fori_loop(1, n_z, gather_step, 0)
    last = at(by_distance(z, n_z - 1, n_z), 1 - x)
    arrived(last)
    project(last)

    gate = acc[0]
    hidden[...] = (gate / (1.0 + jnp.exp(-gate)) * acc[1]).astype(hidden.dtype)

    local[2].wait()
    remote[2].wait_recv()

    def down(part, i):
        b = part * per_part + 2 * i
        cols = [
            jnp.concatenate(
                [downs[slots_out[0, b + k]], downs[slots_out[1, b + k]]], axis=0
            )
            for k in range(2)
        ]
        w = jnp.concatenate(cols, axis=1)
        return jnp.dot(hidden[...], w, preferred_element_type=jnp.float32)

    def lanes(i):
        return pl.ds(pl.multiple_of(i * pair, pair), pair)

    def to_x(dst):
        return send(
            x_out.at[dst], x_in.at[dst], sum_x_send.at[dst], sum_x_recv.at[dst], dev(x_peer)
        )

    def send_x(j, carry):
        dst = by_distance(z, n_z - 1 - j, n_z)

        def step(i, carry):
            x_out[dst, :, lanes(i)] = down(at(dst, 1 - x), i).astype(x_out.dtype)
            return carry

        lax.fori_loop(0, per_part // 2, step, 0)
        to_x(dst).start()
        return carry

    lax.fori_loop(0, n_z, send_x, 0)

    def to_z(dst):
        up = less(z, dst, n_z)
        return send(
            z_out.at[dst], z_in.at[dst, 1 - up], sum_z_send.at[dst], sum_z_recv.at[dst, 1 - up],
            dev(at(z - 1 + 2 * up, x)),
        )

    def from_z(dst, k):
        return send(
            z_out.at[dst], z_in.at[dst, k], sum_z_send.at[dst], sum_z_recv.at[dst, k],
            dev(x_peer),
        )

    def partial_sum(dst, i):
        return down(at(dst, x), i) + x_in[dst, :, lanes(i)].astype(jnp.float32)

    def pass_on(j, carry):
        dst = by_distance(z, n_z - 1 - j, n_z)
        side = 1 - less(z, dst, n_z)
        more = ((dst > z) & (z > 0)) | ((dst < z) & (z < n_z - 1))
        to_x(dst).wait_recv()

        @pl.when(more)
        def _():
            from_z(dst, side).wait_recv()

            def step(i, carry):
                value = partial_sum(dst, i) + z_in[dst, side, :, lanes(i)].astype(jnp.float32)
                z_out[dst, :, lanes(i)] = value.astype(z_out.dtype)
                return carry

            lax.fori_loop(0, per_part // 2, step, 0)

        @pl.when(jnp.logical_not(more))
        def _():
            def step(i, carry):
                z_out[dst, :, lanes(i)] = partial_sum(dst, i).astype(z_out.dtype)
                return carry

            lax.fori_loop(0, per_part // 2, step, 0)

        to_z(dst).start()
        return carry

    lax.fori_loop(0, n_z - 1, pass_on, 0)

    to_x(z).wait_recv()
    side_rows = pl.ds(pl.multiple_of(s * rows, rows), rows)

    @pl.when(z > 0)
    def _():
        from_z(z, 0).wait_recv()

    @pl.when(z < n_z - 1)
    def _():
        from_z(z, 1).wait_recv()

    def finish(use_below, use_above):
        def step(i, carry):
            value = partial_sum(z, i)
            if use_below:
                value += z_in[z, 0, :, lanes(i)].astype(jnp.float32)
            if use_above:
                value += z_in[z, 1, :, lanes(i)].astype(jnp.float32)
            mixed[side_rows, lanes(i)] = value.astype(mixed.dtype)
            return carry

        lax.fori_loop(0, per_part // 2, step, 0)

    @pl.when((z > 0) & (z < n_z - 1))
    def _():
        finish(True, True)

    @pl.when(z == 0)
    def _():
        finish(False, True)

    @pl.when(z == n_z - 1)
    def _():
        finish(True, False)

    swap = send(mixed.at[side_rows], mixed.at[side_rows], mix_sems.at[0], mix_sems.at[1], core_peer)
    swap.start()

    tokens_all = owner.shape[1]
    flags = (owner[...] == s).astype(jnp.float32)
    before = lax.broadcasted_iota(jnp.int32, (tokens_all, tokens_all), 0)
    after = lax.broadcasted_iota(jnp.int32, (tokens_all, tokens_all), 1)
    upto = (before <= after).astype(jnp.bfloat16)
    ranks = jnp.dot(
        jnp.broadcast_to(flags, (8, tokens_all)).astype(jnp.bfloat16),
        upto,
        preferred_element_type=jnp.float32,
    )[0:1]
    places = lax.broadcasted_iota(jnp.int32, (out.shape[0], tokens_all), 0).astype(jnp.float32)
    placing = jnp.where(places + 1.0 == ranks, flags, 0.0).astype(jnp.bfloat16)

    swap.wait_recv()

    def place(i, carry):
        out[:, lanes(i)] = jnp.dot(
            placing, mixed[:, lanes(i)], preferred_element_type=jnp.float32
        ).astype(out.dtype)
        return carry

    lax.fori_loop(0, per_part // 2, place, 0)

    swap.wait_send()
    own_x.wait_send()

    @pl.when(z > 0)
    def _():
        own_to(z - 1, 0).wait_send()

    @pl.when(z < n_z - 1)
    def _():
        own_to(z + 1, 1).wait_send()

    for copy in remote:
        copy.wait_send()

    def drain(j, carry):
        other = by_distance(z, j, n_z)

        @pl.when(goes_on(other))
        def _():
            forward_z(other).wait_send()

        forward_x(other).wait_send()
        to_x(other).wait_send()
        to_z(other).wait_send()
        return carry

    lax.fori_loop(1, n_z, drain, 0)
    to_x(z).wait_send()


def fused(n_tensor, tokens, gate_tiles, up_tiles, down_tiles, in_mask, out_mask, owner_core):
    rows, width = tokens.shape
    half, block, _ = gate_tiles.shape
    n_z, n_x = grid_of(n_tensor)
    cap = 2 * half
    n_hidden = in_mask.shape[0] * block
    kind = tokens.dtype
    everywhere = pl.BlockSpec(memory_space=pl.ANY)
    scalars = pl.BlockSpec(memory_space=pltpu.SMEM)
    vmem = pl.BlockSpec(memory_space=pltpu.VMEM)
    dma = pltpu.SemaphoreType.DMA
    return pl.pallas_call(
        functools.partial(kernel, n_z),
        out_shape=jax.ShapeDtypeStruct((OWN_CAP, width), kind),
        in_specs=[everywhere] * 4 + [scalars] * 2 + [vmem],
        out_specs=vmem,
        scratch_shapes=[
            pltpu.VMEM((n_tensor, rows, width), kind),
            pltpu.VMEM((cap + 1, block, block), kind),
            pltpu.VMEM((cap + 1, block, block), kind),
            pltpu.VMEM((cap + 1, block, block), kind),
            pltpu.SMEM(in_mask.shape, jnp.int32),
            pltpu.SMEM(out_mask.shape, jnp.int32),
            pltpu.VMEM((2, rows, n_hidden), jnp.float32),
            pltpu.VMEM((rows, n_hidden), kind),
            pltpu.VMEM((n_z, rows, width), kind),
            pltpu.VMEM((n_z, rows, width), kind),
            pltpu.VMEM((n_z, rows, width), kind),
            pltpu.VMEM((n_z, 2, rows, width), kind),
            pltpu.VMEM((2 * rows, width), kind),
            dma((3,)),
            dma((3,)),
            dma((3,)),
            dma,
            dma((n_tensor,)),
            dma((3,)),
            dma((n_z,)),
            dma((n_z,)),
            dma((n_z,)),
            dma((n_z,)),
            dma((n_z,)),
            dma((n_z, 2)),
            dma((2,)),
        ],
        compiler_params=pltpu.CompilerParams(
            collective_id=0, has_side_effects=True, vmem_limit_bytes=48 << 20
        ),
    )(tokens, gate_tiles, up_tiles, down_tiles, in_mask, out_mask, owner_core[None, :])


def slot_table(mask_rows, capacity):
    hidden_blocks, width_blocks = mask_rows.shape
    flat_mask = mask_rows.reshape(-1)
    rank_of = jnp.cumsum(flat_mask) - 1
    entries = jnp.arange(hidden_blocks * width_blocks, dtype=jnp.int32)
    slot_ids = jnp.arange(capacity, dtype=jnp.int32)
    matched = ((flat_mask[:, None] == 1) & (rank_of[:, None] == slot_ids[None, :])).astype(
        jnp.int32
    )
    live_flag = jnp.sum(matched, axis=0)
    width_index = jnp.sum(matched * (entries % width_blocks)[:, None], axis=0)
    hidden_index = jnp.sum(matched * (entries // width_blocks)[:, None], axis=0)
    return (width_index, hidden_index, live_flag)


def place_input(tiles, width_index, hidden_index, live_flag, width_blocks, hidden_blocks):
    block_size = tiles.shape[1]
    weighted = tiles * live_flag[:, None, None].astype(tiles.dtype)
    grid_tiles = jnp.zeros((width_blocks, hidden_blocks, block_size, block_size), tiles.dtype)
    grid_tiles = grid_tiles.at[width_index, hidden_index].add(weighted)
    return grid_tiles.transpose(0, 2, 1, 3).reshape(
        width_blocks * block_size, hidden_blocks * block_size
    )


def place_output(tiles, width_index, hidden_index, live_flag, width_blocks, hidden_blocks):
    block_size = tiles.shape[1]
    weighted = tiles * live_flag[:, None, None].astype(tiles.dtype)
    grid_tiles = jnp.zeros((hidden_blocks, width_blocks, block_size, block_size), tiles.dtype)
    grid_tiles = grid_tiles.at[hidden_index, width_index].add(weighted)
    return grid_tiles.transpose(0, 2, 1, 3).reshape(
        hidden_blocks * block_size, width_blocks * block_size
    )


def on_device(tokens, gate_tiles, up_tiles, down_tiles, in_mask, out_mask, owner_core):
    row_count = tokens.shape[0]
    hidden_blocks, width_blocks = in_mask.shape
    core_index = lax.axis_index("seq")
    n_cores = lax.axis_size("seq")
    features = lax.all_gather(tokens, "tensor", axis=1, tiled=True)
    width_in, hidden_in, live_in = slot_table(in_mask, CAP)
    width_out, hidden_out, live_out = slot_table(out_mask, CAP)
    gate_all, up_all, down_all = (
        lax.all_gather(gate_tiles, "seq", axis=0, tiled=True),
        lax.all_gather(up_tiles, "seq", axis=0, tiled=True),
        lax.all_gather(down_tiles, "seq", axis=0, tiled=True),
    )
    w_gate = place_input(gate_all, width_in, hidden_in, live_in, width_blocks, hidden_blocks)
    w_up = place_input(up_all, width_in, hidden_in, live_in, width_blocks, hidden_blocks)
    gate_sum = jnp.dot(features, w_gate, preferred_element_type=jnp.float32)
    up_sum = jnp.dot(features, w_up, preferred_element_type=jnp.float32)
    hidden = (jax.nn.silu(gate_sum) * up_sum).astype(jnp.bfloat16)
    w_down = place_output(down_all, width_out, hidden_out, live_out, width_blocks, hidden_blocks)
    partial_value = jnp.dot(hidden, w_down, preferred_element_type=jnp.float32)
    mixed_rows = lax.psum_scatter(partial_value, "tensor", scatter_dimension=1, tiled=True).astype(
        jnp.bfloat16
    )
    core_ids = jnp.arange(n_cores, dtype=jnp.int32)
    row_ids = jnp.arange(row_count, dtype=jnp.int32)
    local_owner = lax.dynamic_slice_in_dim(owner_core, core_index * row_count, row_count, 0)
    owned_flag = (local_owner[None, :] == core_ids[:, None]).astype(jnp.int32)
    order_in = jnp.cumsum(owned_flag, axis=1) - 1
    packing = (
        (owned_flag[:, None, :] == 1) & (order_in[:, None, :] == row_ids[None, :, None])
    ).astype(jnp.bfloat16)
    outgoing = jnp.einsum(
        "dji,ic->djc", packing, mixed_rows, preferred_element_type=jnp.float32
    ).astype(jnp.bfloat16)
    incoming = lax.all_to_all(outgoing, "seq", split_axis=0, concat_axis=0, tiled=True)
    from_each = jnp.sum(
        (owner_core.reshape(n_cores, row_count) == core_index).astype(jnp.int32), axis=1
    )
    offsets = jnp.cumsum(from_each) - from_each
    target_rows = offsets[:, None] + row_ids[None, :]
    valid_rows = row_ids[None, :] < from_each[:, None]
    out_ids = jnp.arange(OWN_CAP, dtype=jnp.int32)
    placing = ((target_rows[None, :, :] == out_ids[:, None, None]) & valid_rows[None, :, :]).astype(
        jnp.bfloat16
    )
    return jnp.einsum("jsi,sic->jc", placing, incoming, preferred_element_type=jnp.float32).astype(
        jnp.bfloat16
    )


def solution(mesh):
    n_tensor = mesh.shape["tensor"]

    def step(tokens, gate_tiles, up_tiles, down_tiles, in_mask, out_mask, owner_core):
        form = on_device
        if grid_of(n_tensor)[1] == 2 and tokens.shape[1] % (2 * gate_tiles.shape[1]) == 0:
            form = functools.partial(fused, n_tensor)
        return form(tokens, gate_tiles, up_tiles, down_tiles, in_mask, out_mask, owner_core)

    return jax.shard_map(
        step,
        mesh=mesh,
        in_specs=(
            P(("group", "seq"), "tensor"),
            P(("tensor", "seq"), None, None),
            P(("tensor", "seq"), None, None),
            P(("tensor", "seq"), None, None),
            P("tensor", None),
            P("tensor", None),
            P("group"),
        ),
        out_specs=P(("group", "seq"), "tensor"),
        check_vma=False,
    )
```

```python
import functools

import jax
import jax.numpy as jnp
from jax import lax
from jax.experimental import pallas as pl
from jax.experimental.pallas import tpu as pltpu
from jax.sharding import PartitionSpec as P

CAP = 96
OWN_CAP = 192
PIECES = 2
VMEM_LIMIT = 64 << 20
MESH = pl.DeviceIdType.MESH


def grid_of(n_tensor):
    n_x = 1 << ((n_tensor.bit_length() - 1) // 2)
    return n_tensor // n_x, n_x


def less(a, b, n):
    return lax.div(b - a + n, n + 1)


def by_distance(z, j, n_z):
    flip = less(n_z - 1 - z, z, n_z)
    near = z + flip * (n_z - 1 - 2 * z)
    k = lax.div(j + 1, 2)
    both = z + k * (1 - 2 * lax.rem(j, 2))
    one = j + flip * (n_z - 1 - 2 * j)
    far = less(2 * near, j, 2 * n_z)
    return both + far * (one - both)


def kernel(
    n_z,
    pieces,
    tokens,
    gate_tiles,
    up_tiles,
    down_tiles,
    in_mask_hbm,
    out_mask_hbm,
    owner_hbm,
    out,
    feats,
    gates,
    ups,
    downs,
    slots_in,
    slots_out,
    acc,
    hidden,
    x_out,
    x_in,
    z_out,
    z_in,
    side_out,
    side_in,
    mixed,
    in_mask,
    out_mask,
    owner,
    small_copy,
    tile_local,
    tile_send,
    tile_recv,
    own_copy,
    feat_recv,
    own_send,
    feat_z_send,
    feat_x_send,
    peer_send,
    sum_x_send,
    sum_x_recv,
    sum_z_send,
    sum_z_recv,
    side_send,
    side_recv,
    mix_send,
    mix_recv,
):
    t = lax.axis_index("tensor")
    s = lax.axis_index("seq")
    z, x = lax.div(t, 2), lax.rem(t, 2)
    rows = tokens.shape[0]
    span = tokens.shape[1] // pieces
    half, block = gate_tiles.shape[0], gate_tiles.shape[1]
    cap = 2 * half
    n_blocks = in_mask.shape[1]
    per_piece = span // block
    pair = 2 * block
    last = pieces - 1
    has_below, has_above = z > 0, z < n_z - 1

    def dev(tt, ss=None):
        return {"tensor": tt, "seq": s if ss is None else ss}

    def at(zz, xx):
        return zz * 2 + xx

    x_peer = dev(at(z, 1 - x))
    core_peer = dev(t, 1 - s)
    below, above = dev(at(z - 1, x)), dev(at(z + 1, x))

    def send(src, dst, send_sem, recv_sem, device):
        return pltpu.make_async_remote_copy(
            src_ref=src,
            dst_ref=dst,
            send_sem=send_sem,
            recv_sem=recv_sem,
            device_id=device,
            device_id_type=MESH,
        )

    def when(condition, act):
        pl.when(condition)(act)

    barrier = pltpu.get_barrier_semaphore()

    def greet(device):
        pl.semaphore_signal(barrier, inc=1, device_id=device, device_id_type=MESH)

    greet(core_peer)
    greet(x_peer)
    when(has_below, lambda: greet(below))
    when(has_above, lambda: greet(above))

    stacks = ((gate_tiles, gates), (up_tiles, ups), (down_tiles, downs))
    mine = pl.ds(s * half, half)
    smalls = ((in_mask_hbm, in_mask), (out_mask_hbm, out_mask), (owner_hbm, owner))
    small = [pltpu.make_async_copy(*smalls[i], small_copy.at[i]) for i in range(3)]
    for copy in small:
        copy.start()
    own = [
        pltpu.make_async_copy(
            tokens.at[:, pl.ds(p * span, span)], feats.at[t * pieces + p], own_copy.at[p]
        )
        for p in range(pieces)
    ]
    for copy in own:
        copy.start()
    local = [
        pltpu.make_async_copy(src, dst.at[mine], tile_local.at[i])
        for i, (src, dst) in enumerate(stacks)
    ]
    for copy in local:
        copy.start()

    when(has_below & has_above, lambda: pl.semaphore_wait(barrier, 4))
    when(jnp.logical_not(has_below & has_above), lambda: pl.semaphore_wait(barrier, 3))

    def own_to(p, k):
        return send(
            tokens.at[:, pl.ds(p * span, span)],
            feats.at[t * pieces + p],
            own_send.at[k, p],
            feat_recv.at[t * pieces + p],
            (x_peer, below, above)[k],
        )

    for p in range(pieces):
        own_to(p, 0).start()
        when(has_below, lambda: own_to(p, 1).start())
        when(has_above, lambda: own_to(p, 2).start())

    remote = [
        send(src, dst.at[mine], tile_send.at[i], tile_recv.at[i], core_peer)
        for i, (src, dst) in enumerate(stacks)
    ]
    for copy in remote:
        copy.start()

    for dst in (gates, ups, downs):
        dst[cap] = jnp.zeros((block, block), dst.dtype)
    acc[...] = jnp.zeros_like(acc)

    for copy in small:
        copy.wait()
    for mask, table in ((in_mask, slots_in), (out_mask, slots_out)):
        total = jnp.int32(0)
        for c in range(2):

            def fill(b, count, c=c, mask=mask, table=table):
                bit = mask[c, b]
                table[c, b] = jnp.where(bit == 1, count, cap)
                return count + bit

            total = lax.fori_loop(0, n_blocks, fill, total)

    for i in range(2):
        local[i].wait()
        remote[i].wait_recv()

    def lanes(i):
        return pl.ds(pl.multiple_of(i * pair, pair), pair)

    def project(part):
        def step(i, carry):
            b = part * per_piece + 2 * i
            a = feats[part, :, lanes(i)]
            for m, tiles in enumerate((gates, ups)):
                cols = [
                    jnp.concatenate([tiles[slots_in[c, b]], tiles[slots_in[c, b + 1]]], axis=0)
                    for c in range(2)
                ]
                w = jnp.concatenate(cols, axis=1)
                acc[m] += jnp.dot(a, w, preferred_element_type=jnp.float32)
            return carry

        lax.fori_loop(0, per_piece // 2, step, 0)

    def passed(part, sem, device):
        return send(feats.at[part], feats.at[part], sem, feat_recv.at[part], device)

    def arrived(part):
        passed(part, own_send.at[0, 0], x_peer).wait_recv()

    def forward_x(src, p):
        return passed(at(src, x) * pieces + p, feat_x_send.at[src, p], x_peer)

    def forward_z(src, p):
        to = z - 1 + 2 * less(src, z, n_z)
        return passed(at(src, x) * pieces + p, feat_z_send.at[src, p], dev(at(to, x)))

    peer_last = at(z, 1 - x) * pieces + last

    def forward_peer(k):
        return passed(peer_last, peer_send.at[k], (below, above)[k])

    def goes_on(src):
        return ((src < z) & has_above) | ((src > z) & has_below)

    def by_x(other, p):
        near = (other == z - 1) | (other == z + 1)
        return jnp.logical_not(near & (p == last))

    for p in range(pieces):
        own[p].wait()
        project(t * pieces + p)
    for p in range(pieces):
        arrived(at(z, 1 - x) * pieces + p)
        if p == last:
            when(has_below, lambda: forward_peer(0).start())
            when(has_above, lambda: forward_peer(1).start())

    def gather_step(k, carry):
        j, p = lax.div(k, pieces), lax.rem(k, pieces)
        src = by_distance(z, j, n_z)
        arrived(at(src, x) * pieces + p)
        when(goes_on(src), lambda: forward_z(src, p).start())
        when(by_x(src, p), lambda: forward_x(src, p).start())
        before = by_distance(z, j - 1, n_z)
        part = at(before, 1 - x) * pieces + p

        when(j > 1, lambda: arrived(part))
        project(part)
        project(at(src, x) * pieces + p)
        return carry

    lax.fori_loop(pieces, n_z * pieces, gather_step, 0)
    farthest = at(by_distance(z, n_z - 1, n_z), 1 - x) * pieces
    for p in range(pieces):
        arrived(farthest + p)
        project(farthest + p)

    gate = acc[0]
    hidden[...] = (gate / (1.0 + jnp.exp(-gate)) * acc[1]).astype(hidden.dtype)

    local[2].wait()
    remote[2].wait_recv()

    def down(part, i):
        b = part * per_piece + 2 * i
        cols = [
            jnp.concatenate([downs[slots_out[0, b + k]], downs[slots_out[1, b + k]]], axis=0)
            for k in range(2)
        ]
        w = jnp.concatenate(cols, axis=1)
        return jnp.dot(hidden[...], w, preferred_element_type=jnp.float32)

    def each(store):
        def step(i, carry):
            store(i)
            return carry

        lax.fori_loop(0, per_piece // 2, step, 0)

    def wide(value):
        return value.astype(jnp.float32)

    def side_to(k):
        return send(
            side_out.at[k], side_in.at[1 - k], side_send.at[k], side_recv.at[1 - k],
            (below, above)[k],
        )

    def side_go(k):
        dst = z - 1 + 2 * k

        def store(i):
            part = at(dst, 1 - x) * pieces + last
            side_out[k, :, lanes(i)] = down(part, i).astype(side_out.dtype)

        each(store)
        side_to(k).start()

    def to_x(dst, p):
        return send(
            x_out.at[dst, p], x_in.at[dst, p], sum_x_send.at[dst, p], sum_x_recv.at[dst, p], x_peer
        )

    def go_x(dst, p):
        def store(i):
            value = down(at(dst, 1 - x) * pieces + p, i)
            x_out[dst, p, :, lanes(i)] = value.astype(x_out.dtype)

        each(store)
        to_x(dst, p).start()

    def send_x(k, carry):
        j, p = n_z - 1 - lax.div(k, pieces), lax.rem(k, pieces)
        dst = by_distance(z, j, n_z)
        when(by_x(dst, p), lambda: go_x(dst, p))
        return carry

    lax.fori_loop(0, pieces, send_x, 0)
    when(has_below, lambda: side_go(0))
    when(has_above, lambda: side_go(1))
    lax.fori_loop(pieces, n_z * pieces - 1, send_x, 0)

    def go_x_last(use_below, use_above):
        def store(i):
            value = down(at(z, 1 - x) * pieces + last, i)
            if use_below:
                value += wide(side_in[0, :, lanes(i)])
            if use_above:
                value += wide(side_in[1, :, lanes(i)])
            x_out[z, last, :, lanes(i)] = value.astype(x_out.dtype)

        if use_below:
            side_from(0)
        if use_above:
            side_from(1)
        each(store)
        to_x(z, last).start()

    def side_from(k):
        send(
            side_out.at[k], side_in.at[k], side_send.at[k], side_recv.at[k], x_peer
        ).wait_recv()

    def by_place(act):
        when(has_below & has_above, lambda: act(True, True))
        when(z == 0, lambda: act(False, True))
        when(z == n_z - 1, lambda: act(True, False))

    by_place(go_x_last)

    def to_z(dst, p):
        up = less(z, dst, n_z)
        return send(
            z_out.at[dst, p], z_in.at[dst, 1 - up, p], sum_z_send.at[dst, p],
            sum_z_recv.at[dst, 1 - up, p], dev(at(z - 1 + 2 * up, x)),
        )

    def from_z(dst, k, p):
        send(
            z_out.at[dst, p], z_in.at[dst, k, p], sum_z_send.at[dst, p],
            sum_z_recv.at[dst, k, p], x_peer,
        ).wait_recv()

    def pass_on(k, carry):
        j, p = n_z - 1 - lax.div(k, pieces), lax.rem(k, pieces)
        dst = by_distance(z, j, n_z)
        side = 1 - less(z, dst, n_z)
        more = ((dst > z) & has_below) | ((dst < z) & has_above)
        crossed = by_x(dst, p)
        when(crossed, lambda: to_x(dst, p).wait_recv())
        when(more, lambda: from_z(dst, side, p))

        def go(use_x, use_z):
            def store(i):
                value = down(at(dst, x) * pieces + p, i)
                if use_x:
                    value += wide(x_in[dst, p, :, lanes(i)])
                if use_z:
                    value += wide(z_in[dst, side, p, :, lanes(i)])
                z_out[dst, p, :, lanes(i)] = value.astype(z_out.dtype)

            each(store)

        alone = jnp.logical_not(more)
        when(crossed & more, lambda: go(True, True))
        when(crossed & alone, lambda: go(True, False))
        when(jnp.logical_not(crossed) & more, lambda: go(False, True))
        when(jnp.logical_not(crossed) & alone, lambda: go(False, False))
        to_z(dst, p).start()
        return carry

    lax.fori_loop(0, (n_z - 1) * pieces, pass_on, 0)

    mine = pl.ds(pl.multiple_of(s * rows, rows), rows)

    def swap(p):
        return send(
            mixed.at[p, mine], mixed.at[p, mine], mix_send.at[p], mix_recv.at[p], core_peer
        )

    def finish(p, use_below, use_above):
        def store(i):
            value = down(t * pieces + p, i) + wide(x_in[z, p, :, lanes(i)])
            if use_below:
                value += wide(z_in[z, 0, p, :, lanes(i)])
            if use_above:
                value += wide(z_in[z, 1, p, :, lanes(i)])
            mixed[p, mine, lanes(i)] = value.astype(mixed.dtype)

        if use_below:
            from_z(z, 0, p)
        if use_above:
            from_z(z, 1, p)
        each(store)

    tokens_all = owner.shape[1]
    flags = (owner[...] == s).astype(jnp.float32)
    first = lax.broadcasted_iota(jnp.int32, (tokens_all, tokens_all), 0)
    second = lax.broadcasted_iota(jnp.int32, (tokens_all, tokens_all), 1)
    upto = (first <= second).astype(jnp.bfloat16)
    ranks = jnp.dot(
        jnp.broadcast_to(flags, (8, tokens_all)).astype(jnp.bfloat16),
        upto,
        preferred_element_type=jnp.float32,
    )[0:1]
    places = lax.broadcasted_iota(jnp.int32, (out.shape[0], tokens_all), 0).astype(jnp.float32)
    placing = jnp.where(places + 1.0 == ranks, flags, 0.0).astype(jnp.bfloat16)

    for p in range(pieces):
        to_x(z, p).wait_recv()
        by_place(functools.partial(finish, p))
        swap(p).start()

    for p in range(pieces):
        swap(p).wait_recv()
        for i in range(per_piece // 2):
            out[:, pl.ds(p * span + i * pair, pair)] = jnp.dot(
                placing, mixed[p, :, pl.ds(i * pair, pair)], preferred_element_type=jnp.float32
            ).astype(out.dtype)

    for p in range(pieces):
        swap(p).wait_send()
        own_to(p, 0).wait_send()
        when(has_below, lambda: own_to(p, 1).wait_send())
        when(has_above, lambda: own_to(p, 2).wait_send())
        to_x(z, p).wait_send()
    for k, there in enumerate((has_below, has_above)):
        when(there, lambda: forward_peer(k).wait_send())
        when(there, lambda: side_to(k).wait_send())
    for copy in remote:
        copy.wait_send()

    def drain(k, carry):
        j, p = lax.div(k, pieces), lax.rem(k, pieces)
        other = by_distance(z, j, n_z)
        when(goes_on(other), lambda: forward_z(other, p).wait_send())
        when(by_x(other, p), lambda: forward_x(other, p).wait_send())
        when(by_x(other, p), lambda: to_x(other, p).wait_send())
        to_z(other, p).wait_send()
        return carry

    lax.fori_loop(pieces, n_z * pieces, drain, 0)


def fused(n_tensor, tokens, gate_tiles, up_tiles, down_tiles, in_mask, out_mask, owner_core):
    rows, width = tokens.shape
    half, block, _ = gate_tiles.shape
    n_z, n_x = grid_of(n_tensor)
    pieces = PIECES
    span = width // pieces
    cap = 2 * half
    n_hidden = in_mask.shape[0] * block
    kind = tokens.dtype
    hbm = pl.BlockSpec(memory_space=pltpu.HBM)
    vmem = pl.BlockSpec(memory_space=pltpu.VMEM)
    dma = pltpu.SemaphoreType.DMA
    return pl.pallas_call(
        functools.partial(kernel, n_z, pieces),
        out_shape=jax.ShapeDtypeStruct((OWN_CAP, width), kind),
        in_specs=[hbm] * 7,
        out_specs=vmem,
        scratch_shapes=[
            pltpu.VMEM((n_tensor * pieces, rows, span), kind),
            pltpu.VMEM((cap + 1, block, block), kind),
            pltpu.VMEM((cap + 1, block, block), kind),
            pltpu.VMEM((cap + 1, block, block), kind),
            pltpu.SMEM(in_mask.shape, jnp.int32),
            pltpu.SMEM(out_mask.shape, jnp.int32),
            pltpu.VMEM((2, rows, n_hidden), jnp.float32),
            pltpu.VMEM((rows, n_hidden), kind),
            pltpu.VMEM((n_z, pieces, rows, span), kind),
            pltpu.VMEM((n_z, pieces, rows, span), kind),
            pltpu.VMEM((n_z, pieces, rows, span), kind),
            pltpu.VMEM((n_z, 2, pieces, rows, span), kind),
            pltpu.VMEM((2, rows, span), kind),
            pltpu.VMEM((2, rows, span), kind),
            pltpu.VMEM((pieces, 2 * rows, span), kind),
            pltpu.SMEM(in_mask.shape, jnp.int32),
            pltpu.SMEM(out_mask.shape, jnp.int32),
            pltpu.VMEM((1,) + owner_core.shape, jnp.int32),
            dma((3,)),
            dma((3,)),
            dma((3,)),
            dma((3,)),
            dma((pieces,)),
            dma((n_tensor * pieces,)),
            dma((3, pieces)),
            dma((n_z, pieces)),
            dma((n_z, pieces)),
            dma((2,)),
            dma((n_z, pieces)),
            dma((n_z, pieces)),
            dma((n_z, pieces)),
            dma((n_z, 2, pieces)),
            dma((2,)),
            dma((2,)),
            dma((pieces,)),
            dma((pieces,)),
        ],
        compiler_params=pltpu.CompilerParams(
            collective_id=0, has_side_effects=True, vmem_limit_bytes=VMEM_LIMIT
        ),
    )(tokens, gate_tiles, up_tiles, down_tiles, in_mask, out_mask, owner_core[None, :])


def slot_table(mask_rows, capacity):
    hidden_blocks, width_blocks = mask_rows.shape
    flat_mask = mask_rows.reshape(-1)
    rank_of = jnp.cumsum(flat_mask) - 1
    entries = jnp.arange(hidden_blocks * width_blocks, dtype=jnp.int32)
    slot_ids = jnp.arange(capacity, dtype=jnp.int32)
    matched = ((flat_mask[:, None] == 1) & (rank_of[:, None] == slot_ids[None, :])).astype(
        jnp.int32
    )
    live_flag = jnp.sum(matched, axis=0)
    width_index = jnp.sum(matched * (entries % width_blocks)[:, None], axis=0)
    hidden_index = jnp.sum(matched * (entries // width_blocks)[:, None], axis=0)
    return (width_index, hidden_index, live_flag)


def place_input(tiles, width_index, hidden_index, live_flag, width_blocks, hidden_blocks):
    block_size = tiles.shape[1]
    weighted = tiles * live_flag[:, None, None].astype(tiles.dtype)
    grid_tiles = jnp.zeros((width_blocks, hidden_blocks, block_size, block_size), tiles.dtype)
    grid_tiles = grid_tiles.at[width_index, hidden_index].add(weighted)
    return grid_tiles.transpose(0, 2, 1, 3).reshape(
        width_blocks * block_size, hidden_blocks * block_size
    )


def place_output(tiles, width_index, hidden_index, live_flag, width_blocks, hidden_blocks):
    block_size = tiles.shape[1]
    weighted = tiles * live_flag[:, None, None].astype(tiles.dtype)
    grid_tiles = jnp.zeros((hidden_blocks, width_blocks, block_size, block_size), tiles.dtype)
    grid_tiles = grid_tiles.at[hidden_index, width_index].add(weighted)
    return grid_tiles.transpose(0, 2, 1, 3).reshape(
        hidden_blocks * block_size, width_blocks * block_size
    )


def on_device(tokens, gate_tiles, up_tiles, down_tiles, in_mask, out_mask, owner_core):
    row_count = tokens.shape[0]
    hidden_blocks, width_blocks = in_mask.shape
    core_index = lax.axis_index("seq")
    n_cores = lax.axis_size("seq")
    features = lax.all_gather(tokens, "tensor", axis=1, tiled=True)
    width_in, hidden_in, live_in = slot_table(in_mask, CAP)
    width_out, hidden_out, live_out = slot_table(out_mask, CAP)
    gate_all, up_all, down_all = (
        lax.all_gather(gate_tiles, "seq", axis=0, tiled=True),
        lax.all_gather(up_tiles, "seq", axis=0, tiled=True),
        lax.all_gather(down_tiles, "seq", axis=0, tiled=True),
    )
    w_gate = place_input(gate_all, width_in, hidden_in, live_in, width_blocks, hidden_blocks)
    w_up = place_input(up_all, width_in, hidden_in, live_in, width_blocks, hidden_blocks)
    gate_sum = jnp.dot(features, w_gate, preferred_element_type=jnp.float32)
    up_sum = jnp.dot(features, w_up, preferred_element_type=jnp.float32)
    hidden = (jax.nn.silu(gate_sum) * up_sum).astype(jnp.bfloat16)
    w_down = place_output(down_all, width_out, hidden_out, live_out, width_blocks, hidden_blocks)
    partial_value = jnp.dot(hidden, w_down, preferred_element_type=jnp.float32)
    mixed_rows = lax.psum_scatter(partial_value, "tensor", scatter_dimension=1, tiled=True).astype(
        jnp.bfloat16
    )
    core_ids = jnp.arange(n_cores, dtype=jnp.int32)
    row_ids = jnp.arange(row_count, dtype=jnp.int32)
    local_owner = lax.dynamic_slice_in_dim(owner_core, core_index * row_count, row_count, 0)
    owned_flag = (local_owner[None, :] == core_ids[:, None]).astype(jnp.int32)
    order_in = jnp.cumsum(owned_flag, axis=1) - 1
    packing = (
        (owned_flag[:, None, :] == 1) & (order_in[:, None, :] == row_ids[None, :, None])
    ).astype(jnp.bfloat16)
    outgoing = jnp.einsum(
        "dji,ic->djc", packing, mixed_rows, preferred_element_type=jnp.float32
    ).astype(jnp.bfloat16)
    incoming = lax.all_to_all(outgoing, "seq", split_axis=0, concat_axis=0, tiled=True)
    from_each = jnp.sum(
        (owner_core.reshape(n_cores, row_count) == core_index).astype(jnp.int32), axis=1
    )
    offsets = jnp.cumsum(from_each) - from_each
    target_rows = offsets[:, None] + row_ids[None, :]
    valid_rows = row_ids[None, :] < from_each[:, None]
    out_ids = jnp.arange(OWN_CAP, dtype=jnp.int32)
    placing = ((target_rows[None, :, :] == out_ids[:, None, None]) & valid_rows[None, :, :]).astype(
        jnp.bfloat16
    )
    return jnp.einsum("jsi,sic->jc", placing, incoming, preferred_element_type=jnp.float32).astype(
        jnp.bfloat16
    )


def solution(mesh):
    n_tensor = mesh.shape["tensor"]

    def step(tokens, gate_tiles, up_tiles, down_tiles, in_mask, out_mask, owner_core):
        form = on_device
        if grid_of(n_tensor)[1] == 2 and tokens.shape[1] % (2 * PIECES * gate_tiles.shape[1]) == 0:
            form = functools.partial(fused, n_tensor)
        return form(tokens, gate_tiles, up_tiles, down_tiles, in_mask, out_mask, owner_core)

    return jax.shard_map(
        step,
        mesh=mesh,
        in_specs=(
            P(("group", "seq"), "tensor"),
            P(("tensor", "seq"), None, None),
            P(("tensor", "seq"), None, None),
            P(("tensor", "seq"), None, None),
            P("tensor", None),
            P("tensor", None),
            P("group"),
        ),
        out_specs=P(("group", "seq"), "tensor"),
        check_vma=False,
    )
```

```python
import functools

import jax
import jax.numpy as jnp
from jax import lax
from jax.experimental import pallas as pl
from jax.experimental.pallas import tpu as pltpu
from jax.sharding import PartitionSpec as P

CAP = 96
OWN_CAP = 192
PIECES = 2
SIDE = 1
VMEM_LIMIT = 64 << 20
MESH = pl.DeviceIdType.MESH


def grid_of(n_tensor):
    n_x = 1 << ((n_tensor.bit_length() - 1) // 2)
    return n_tensor // n_x, n_x


def less(a, b, n):
    return lax.div(b - a + n, n + 1)


def by_distance(z, j, n_z):
    flip = less(n_z - 1 - z, z, n_z)
    near = z + flip * (n_z - 1 - 2 * z)
    k = lax.div(j + 1, 2)
    both = z + k * (1 - 2 * lax.rem(j, 2))
    one = j + flip * (n_z - 1 - 2 * j)
    far = less(2 * near, j, 2 * n_z)
    return both + far * (one - both)


def kernel(
    n_z,
    pieces,
    tokens,
    gate_tiles,
    up_tiles,
    down_tiles,
    in_mask_hbm,
    out_mask_hbm,
    owner_hbm,
    out,
    feats,
    gates,
    ups,
    downs,
    slots_in,
    slots_out,
    acc,
    hidden,
    x_out,
    x_in,
    z_out,
    z_in,
    side_out,
    side_in,
    mixed,
    in_mask,
    out_mask,
    owner,
    small_copy,
    tile_local,
    tile_send,
    tile_recv,
    own_copy,
    feat_recv,
    own_send,
    feat_z_send,
    feat_x_send,
    peer_send,
    sum_x_send,
    sum_x_recv,
    sum_z_send,
    sum_z_recv,
    side_send,
    side_recv,
    mix_send,
    mix_recv,
):
    t = lax.axis_index("tensor")
    s = lax.axis_index("seq")
    z, x = lax.div(t, 2), lax.rem(t, 2)
    rows = tokens.shape[0]
    span = tokens.shape[1] // pieces
    half, block = gate_tiles.shape[0], gate_tiles.shape[1]
    cap = 2 * half
    n_blocks = in_mask.shape[1]
    per_piece = span // block
    pair = 2 * block
    straight = pieces - SIDE
    has_below, has_above = z > 0, z < n_z - 1

    def dev(tt, ss=None):
        return {"tensor": tt, "seq": s if ss is None else ss}

    def at(zz, xx):
        return zz * 2 + xx

    x_peer = dev(at(z, 1 - x))
    core_peer = dev(t, 1 - s)
    below, above = dev(at(z - 1, x)), dev(at(z + 1, x))

    def send(src, dst, send_sem, recv_sem, device):
        return pltpu.make_async_remote_copy(
            src_ref=src,
            dst_ref=dst,
            send_sem=send_sem,
            recv_sem=recv_sem,
            device_id=device,
            device_id_type=MESH,
        )

    def when(condition, act):
        pl.when(condition)(act)

    barrier = pltpu.get_barrier_semaphore()

    def greet(device):
        pl.semaphore_signal(barrier, inc=1, device_id=device, device_id_type=MESH)

    greet(core_peer)
    greet(x_peer)
    when(has_below, lambda: greet(below))
    when(has_above, lambda: greet(above))

    stacks = ((gate_tiles, gates), (up_tiles, ups), (down_tiles, downs))
    mine = pl.ds(s * half, half)
    smalls = ((in_mask_hbm, in_mask), (out_mask_hbm, out_mask), (owner_hbm, owner))
    small = [pltpu.make_async_copy(*smalls[i], small_copy.at[i]) for i in range(3)]
    for copy in small:
        copy.start()
    own = [
        pltpu.make_async_copy(
            tokens.at[:, pl.ds(p * span, span)], feats.at[t * pieces + p], own_copy.at[p]
        )
        for p in range(pieces)
    ]
    for copy in own:
        copy.start()
    local = [
        pltpu.make_async_copy(src, dst.at[mine], tile_local.at[i])
        for i, (src, dst) in enumerate(stacks)
    ]
    for copy in local:
        copy.start()

    when(has_below & has_above, lambda: pl.semaphore_wait(barrier, 4))
    when(jnp.logical_not(has_below & has_above), lambda: pl.semaphore_wait(barrier, 3))

    def own_to(p, k):
        return send(
            feats.at[t * pieces + p],
            feats.at[t * pieces + p],
            own_send.at[k, p],
            feat_recv.at[t * pieces + p],
            (x_peer, below, above)[k],
        )

    for p in range(pieces):
        own[p].wait()
        own_to(p, 0).start()
        when(has_below, lambda: own_to(p, 1).start())
        when(has_above, lambda: own_to(p, 2).start())

    remote = [
        send(src, dst.at[mine], tile_send.at[i], tile_recv.at[i], core_peer)
        for i, (src, dst) in enumerate(stacks)
    ]
    for copy in remote:
        copy.start()

    for dst in (gates, ups, downs):
        dst[cap] = jnp.zeros((block, block), dst.dtype)
    acc[...] = jnp.zeros_like(acc)

    def number(mask, table):
        total = jnp.int32(0)
        for c in range(2):

            def fill(b, count, c=c):
                bit = mask[c, b]
                table[c, b] = jnp.where(bit == 1, count, cap)
                return count + bit

            total = lax.fori_loop(0, n_blocks, fill, total)

    small[0].wait()
    number(in_mask, slots_in)

    def lanes(i):
        return pl.ds(pl.multiple_of(i * pair, pair), pair)

    def project(part):
        def step(i, carry):
            b = part * per_piece + 2 * i
            a = feats[part, :, lanes(i)]
            for m, tiles in enumerate((gates, ups)):
                cols = [
                    jnp.concatenate([tiles[slots_in[c, b]], tiles[slots_in[c, b + 1]]], axis=0)
                    for c in range(2)
                ]
                w = jnp.concatenate(cols, axis=1)
                acc[m] += jnp.dot(a, w, preferred_element_type=jnp.float32)
            return carry

        lax.fori_loop(0, per_piece // 2, step, 0)

    def passed(part, sem, device):
        return send(feats.at[part], feats.at[part], sem, feat_recv.at[part], device)

    def arrived(part):
        passed(part, own_send.at[0, 0], x_peer).wait_recv()

    def forward_x(src, p):
        return passed(at(src, x) * pieces + p, feat_x_send.at[src, p], x_peer)

    def forward_z(src, p):
        to = z - 1 + 2 * less(src, z, n_z)
        return passed(at(src, x) * pieces + p, feat_z_send.at[src, p], dev(at(to, x)))

    def forward_peer(k, p):
        part = at(z, 1 - x) * pieces + p
        return passed(part, peer_send.at[k, p - straight], (below, above)[k])

    def goes_on(src):
        return ((src < z) & has_above) | ((src > z) & has_below)

    def by_x(other, p):
        near = (other == z - 1) | (other == z + 1)
        return jnp.logical_not(near & (p >= straight))

    def take(src, p):
        arrived(at(src, x) * pieces + p)
        when(goes_on(src), lambda: forward_z(src, p).start())
        when(by_x(src, p), lambda: forward_x(src, p).start())

    for p in range(pieces):
        when(has_below, lambda: take(z - 1, p))
        when(has_above, lambda: take(z + 1, p))
        arrived(at(z, 1 - x) * pieces + p)
        if p >= straight:
            when(has_below, lambda: forward_peer(0, p).start())
            when(has_above, lambda: forward_peer(1, p).start())

    for i in range(2):
        local[i].wait()
        remote[i].wait_recv()
    def near_products(p, carry):
        project(t * pieces + p)
        project(at(z, 1 - x) * pieces + p)
        when(has_below, lambda: project(at(z - 1, x) * pieces + p))
        when(has_above, lambda: project(at(z + 1, x) * pieces + p))
        return carry

    lax.fori_loop(0, pieces, near_products, 0)

    def gather_step(k, carry):
        j, p = lax.div(k, pieces), lax.rem(k, pieces)
        src = by_distance(z, j, n_z)
        far = jnp.logical_not((src == z - 1) | (src == z + 1))
        when(far, lambda: take(src, p))
        before = at(by_distance(z, j - 1, n_z), 1 - x) * pieces + p
        arrived(before)
        project(before)
        when(far, lambda: project(at(src, x) * pieces + p))
        return carry

    lax.fori_loop(2 * pieces, n_z * pieces, gather_step, 0)
    small[1].wait()
    number(out_mask, slots_out)
    farthest = at(by_distance(z, n_z - 1, n_z), 1 - x) * pieces
    for p in range(pieces):
        arrived(farthest + p)
        project(farthest + p)

    gate = acc[0]
    hidden[...] = (gate / (1.0 + jnp.exp(-gate)) * acc[1]).astype(hidden.dtype)

    local[2].wait()
    remote[2].wait_recv()

    def down(part, i):
        b = part * per_piece + 2 * i
        cols = [
            jnp.concatenate([downs[slots_out[0, b + k]], downs[slots_out[1, b + k]]], axis=0)
            for k in range(2)
        ]
        w = jnp.concatenate(cols, axis=1)
        return jnp.dot(hidden[...], w, preferred_element_type=jnp.float32)

    def each(store):
        def step(i, carry):
            store(i)
            return carry

        lax.fori_loop(0, per_piece // 2, step, 0)

    def wide(value):
        return value.astype(jnp.float32)

    def side_to(k, p):
        q = p - straight
        return send(
            side_out.at[k, q], side_in.at[1 - k, q], side_send.at[k, q], side_recv.at[1 - k, q],
            (below, above)[k],
        )

    def side_from(k, p):
        q = p - straight
        send(
            side_out.at[k, q], side_in.at[k, q], side_send.at[k, q], side_recv.at[k, q], x_peer
        ).wait_recv()

    def side_go(k, p):
        dst = z - 1 + 2 * k

        def store(i):
            value = down(at(dst, 1 - x) * pieces + p, i)
            side_out[k, p - straight, :, lanes(i)] = value.astype(side_out.dtype)

        each(store)
        side_to(k, p).start()

    def to_x(dst, p):
        return send(
            x_out.at[dst, p], x_in.at[dst, p], sum_x_send.at[dst, p], sum_x_recv.at[dst, p], x_peer
        )

    def go_x(dst, p):
        def store(i):
            value = down(at(dst, 1 - x) * pieces + p, i)
            x_out[dst, p, :, lanes(i)] = value.astype(x_out.dtype)

        each(store)
        to_x(dst, p).start()

    def send_x(k, carry):
        j, p = n_z - 1 - lax.div(k, pieces), lax.rem(k, pieces)
        dst = by_distance(z, j, n_z)
        when(by_x(dst, p), lambda: go_x(dst, p))
        return carry

    lax.fori_loop(0, 2, send_x, 0)
    for p in range(straight, pieces):
        when(has_below, lambda: side_go(0, p))
        when(has_above, lambda: side_go(1, p))
    lax.fori_loop(2, n_z * pieces - SIDE, send_x, 0)

    def go_x_last(p, use_below, use_above):
        def store(i):
            value = down(at(z, 1 - x) * pieces + p, i)
            if use_below:
                value += wide(side_in[0, p - straight, :, lanes(i)])
            if use_above:
                value += wide(side_in[1, p - straight, :, lanes(i)])
            x_out[z, p, :, lanes(i)] = value.astype(x_out.dtype)

        if use_below:
            side_from(0, p)
        if use_above:
            side_from(1, p)
        each(store)
        to_x(z, p).start()

    def by_place(act):
        when(has_below & has_above, lambda: act(True, True))
        when(z == 0, lambda: act(False, True))
        when(z == n_z - 1, lambda: act(True, False))


    def to_z(dst, p):
        up = less(z, dst, n_z)
        return send(
            z_out.at[dst, p], z_in.at[dst, 1 - up, p], sum_z_send.at[dst, p],
            sum_z_recv.at[dst, 1 - up, p], dev(at(z - 1 + 2 * up, x)),
        )

    def from_z(dst, k, p):
        send(
            z_out.at[dst, p], z_in.at[dst, k, p], sum_z_send.at[dst, p],
            sum_z_recv.at[dst, k, p], x_peer,
        ).wait_recv()

    def pass_on(k, carry):
        j, p = n_z - 1 - lax.div(k, pieces), lax.rem(k, pieces)
        dst = by_distance(z, j, n_z)
        side = 1 - less(z, dst, n_z)
        more = ((dst > z) & has_below) | ((dst < z) & has_above)
        crossed = by_x(dst, p)
        when(crossed, lambda: to_x(dst, p).wait_recv())
        when(more, lambda: from_z(dst, side, p))

        def go(use_x, use_z):
            def store(i):
                value = down(at(dst, x) * pieces + p, i)
                if use_x:
                    value += wide(x_in[dst, p, :, lanes(i)])
                if use_z:
                    value += wide(z_in[dst, side, p, :, lanes(i)])
                z_out[dst, p, :, lanes(i)] = value.astype(z_out.dtype)

            each(store)

        alone = jnp.logical_not(more)
        when(crossed & more, lambda: go(True, True))
        when(crossed & alone, lambda: go(True, False))
        when(jnp.logical_not(crossed) & more, lambda: go(False, True))
        when(jnp.logical_not(crossed) & alone, lambda: go(False, False))
        to_z(dst, p).start()
        return carry

    lax.fori_loop(0, pieces, pass_on, 0)
    for p in range(straight, pieces):
        by_place(functools.partial(go_x_last, p))
    lax.fori_loop(pieces, (n_z - 1) * pieces, pass_on, 0)

    mine = pl.ds(pl.multiple_of(s * rows, rows), rows)

    def swap(p):
        return send(
            mixed.at[p, mine], mixed.at[p, mine], mix_send.at[p], mix_recv.at[p], core_peer
        )

    def finish(p, use_below, use_above):
        def store(i):
            value = down(t * pieces + p, i) + wide(x_in[z, p, :, lanes(i)])
            if use_below:
                value += wide(z_in[z, 0, p, :, lanes(i)])
            if use_above:
                value += wide(z_in[z, 1, p, :, lanes(i)])
            mixed[p, mine, lanes(i)] = value.astype(mixed.dtype)

        if use_below:
            from_z(z, 0, p)
        if use_above:
            from_z(z, 1, p)
        each(store)

    small[2].wait()
    tokens_all = owner.shape[1]
    flags = (owner[...] == s).astype(jnp.float32)
    first = lax.broadcasted_iota(jnp.int32, (tokens_all, tokens_all), 0)
    second = lax.broadcasted_iota(jnp.int32, (tokens_all, tokens_all), 1)
    upto = (first <= second).astype(jnp.bfloat16)
    ranks = jnp.dot(
        jnp.broadcast_to(flags, (8, tokens_all)).astype(jnp.bfloat16),
        upto,
        preferred_element_type=jnp.float32,
    )[0:1]
    places = lax.broadcasted_iota(jnp.int32, (out.shape[0], tokens_all), 0).astype(jnp.float32)
    placing = jnp.where(places + 1.0 == ranks, flags, 0.0).astype(jnp.bfloat16)

    for p in range(pieces):
        to_x(z, p).wait_recv()
        by_place(functools.partial(finish, p))
        swap(p).start()

    for p in range(pieces):
        swap(p).wait_recv()
        for i in range(per_piece // 2):
            out[:, pl.ds(p * span + i * pair, pair)] = jnp.dot(
                placing, mixed[p, :, pl.ds(i * pair, pair)], preferred_element_type=jnp.float32
            ).astype(out.dtype)

    for p in range(pieces):
        swap(p).wait_send()
        own_to(p, 0).wait_send()
        when(has_below, lambda: own_to(p, 1).wait_send())
        when(has_above, lambda: own_to(p, 2).wait_send())
        to_x(z, p).wait_send()
    for k, there in enumerate((has_below, has_above)):
        for p in range(straight, pieces):
            when(there, lambda: forward_peer(k, p).wait_send())
            when(there, lambda: side_to(k, p).wait_send())
    for copy in remote:
        copy.wait_send()

    def drain(k, carry):
        j, p = lax.div(k, pieces), lax.rem(k, pieces)
        other = by_distance(z, j, n_z)
        when(goes_on(other), lambda: forward_z(other, p).wait_send())
        when(by_x(other, p), lambda: forward_x(other, p).wait_send())
        when(by_x(other, p), lambda: to_x(other, p).wait_send())
        to_z(other, p).wait_send()
        return carry

    lax.fori_loop(pieces, n_z * pieces, drain, 0)


def fused(n_tensor, tokens, gate_tiles, up_tiles, down_tiles, in_mask, out_mask, owner_core):
    rows, width = tokens.shape
    half, block, _ = gate_tiles.shape
    n_z, n_x = grid_of(n_tensor)
    pieces = PIECES
    span = width // pieces
    cap = 2 * half
    n_hidden = in_mask.shape[0] * block
    kind = tokens.dtype
    hbm = pl.BlockSpec(memory_space=pltpu.HBM)
    vmem = pl.BlockSpec(memory_space=pltpu.VMEM)
    dma = pltpu.SemaphoreType.DMA
    return pl.pallas_call(
        functools.partial(kernel, n_z, pieces),
        out_shape=jax.ShapeDtypeStruct((OWN_CAP, width), kind),
        in_specs=[hbm] * 7,
        out_specs=vmem,
        scratch_shapes=[
            pltpu.VMEM((n_tensor * pieces, rows, span), kind),
            pltpu.VMEM((cap + 1, block, block), kind),
            pltpu.VMEM((cap + 1, block, block), kind),
            pltpu.VMEM((cap + 1, block, block), kind),
            pltpu.SMEM(in_mask.shape, jnp.int32),
            pltpu.SMEM(out_mask.shape, jnp.int32),
            pltpu.VMEM((2, rows, n_hidden), jnp.float32),
            pltpu.VMEM((rows, n_hidden), kind),
            pltpu.VMEM((n_z, pieces, rows, span), kind),
            pltpu.VMEM((n_z, pieces, rows, span), kind),
            pltpu.VMEM((n_z, pieces, rows, span), kind),
            pltpu.VMEM((n_z, 2, pieces, rows, span), kind),
            pltpu.VMEM((2, SIDE, rows, span), kind),
            pltpu.VMEM((2, SIDE, rows, span), kind),
            pltpu.VMEM((pieces, 2 * rows, span), kind),
            pltpu.SMEM(in_mask.shape, jnp.int32),
            pltpu.SMEM(out_mask.shape, jnp.int32),
            pltpu.VMEM((1,) + owner_core.shape, jnp.int32),
            dma((3,)),
            dma((3,)),
            dma((3,)),
            dma((3,)),
            dma((pieces,)),
            dma((n_tensor * pieces,)),
            dma((3, pieces)),
            dma((n_z, pieces)),
            dma((n_z, pieces)),
            dma((2, SIDE)),
            dma((n_z, pieces)),
            dma((n_z, pieces)),
            dma((n_z, pieces)),
            dma((n_z, 2, pieces)),
            dma((2, SIDE)),
            dma((2, SIDE)),
            dma((pieces,)),
            dma((pieces,)),
        ],
        compiler_params=pltpu.CompilerParams(
            collective_id=0, has_side_effects=True, vmem_limit_bytes=VMEM_LIMIT
        ),
    )(tokens, gate_tiles, up_tiles, down_tiles, in_mask, out_mask, owner_core[None, :])


def slot_table(mask_rows, capacity):
    hidden_blocks, width_blocks = mask_rows.shape
    flat_mask = mask_rows.reshape(-1)
    rank_of = jnp.cumsum(flat_mask) - 1
    entries = jnp.arange(hidden_blocks * width_blocks, dtype=jnp.int32)
    slot_ids = jnp.arange(capacity, dtype=jnp.int32)
    matched = ((flat_mask[:, None] == 1) & (rank_of[:, None] == slot_ids[None, :])).astype(
        jnp.int32
    )
    live_flag = jnp.sum(matched, axis=0)
    width_index = jnp.sum(matched * (entries % width_blocks)[:, None], axis=0)
    hidden_index = jnp.sum(matched * (entries // width_blocks)[:, None], axis=0)
    return (width_index, hidden_index, live_flag)


def place_input(tiles, width_index, hidden_index, live_flag, width_blocks, hidden_blocks):
    block_size = tiles.shape[1]
    weighted = tiles * live_flag[:, None, None].astype(tiles.dtype)
    grid_tiles = jnp.zeros((width_blocks, hidden_blocks, block_size, block_size), tiles.dtype)
    grid_tiles = grid_tiles.at[width_index, hidden_index].add(weighted)
    return grid_tiles.transpose(0, 2, 1, 3).reshape(
        width_blocks * block_size, hidden_blocks * block_size
    )


def place_output(tiles, width_index, hidden_index, live_flag, width_blocks, hidden_blocks):
    block_size = tiles.shape[1]
    weighted = tiles * live_flag[:, None, None].astype(tiles.dtype)
    grid_tiles = jnp.zeros((hidden_blocks, width_blocks, block_size, block_size), tiles.dtype)
    grid_tiles = grid_tiles.at[hidden_index, width_index].add(weighted)
    return grid_tiles.transpose(0, 2, 1, 3).reshape(
        hidden_blocks * block_size, width_blocks * block_size
    )


def on_device(tokens, gate_tiles, up_tiles, down_tiles, in_mask, out_mask, owner_core):
    row_count = tokens.shape[0]
    hidden_blocks, width_blocks = in_mask.shape
    core_index = lax.axis_index("seq")
    n_cores = lax.axis_size("seq")
    features = lax.all_gather(tokens, "tensor", axis=1, tiled=True)
    width_in, hidden_in, live_in = slot_table(in_mask, CAP)
    width_out, hidden_out, live_out = slot_table(out_mask, CAP)
    gate_all, up_all, down_all = (
        lax.all_gather(gate_tiles, "seq", axis=0, tiled=True),
        lax.all_gather(up_tiles, "seq", axis=0, tiled=True),
        lax.all_gather(down_tiles, "seq", axis=0, tiled=True),
    )
    w_gate = place_input(gate_all, width_in, hidden_in, live_in, width_blocks, hidden_blocks)
    w_up = place_input(up_all, width_in, hidden_in, live_in, width_blocks, hidden_blocks)
    gate_sum = jnp.dot(features, w_gate, preferred_element_type=jnp.float32)
    up_sum = jnp.dot(features, w_up, preferred_element_type=jnp.float32)
    hidden = (jax.nn.silu(gate_sum) * up_sum).astype(jnp.bfloat16)
    w_down = place_output(down_all, width_out, hidden_out, live_out, width_blocks, hidden_blocks)
    partial_value = jnp.dot(hidden, w_down, preferred_element_type=jnp.float32)
    mixed_rows = lax.psum_scatter(partial_value, "tensor", scatter_dimension=1, tiled=True).astype(
        jnp.bfloat16
    )
    core_ids = jnp.arange(n_cores, dtype=jnp.int32)
    row_ids = jnp.arange(row_count, dtype=jnp.int32)
    local_owner = lax.dynamic_slice_in_dim(owner_core, core_index * row_count, row_count, 0)
    owned_flag = (local_owner[None, :] == core_ids[:, None]).astype(jnp.int32)
    order_in = jnp.cumsum(owned_flag, axis=1) - 1
    packing = (
        (owned_flag[:, None, :] == 1) & (order_in[:, None, :] == row_ids[None, :, None])
    ).astype(jnp.bfloat16)
    outgoing = jnp.einsum(
        "dji,ic->djc", packing, mixed_rows, preferred_element_type=jnp.float32
    ).astype(jnp.bfloat16)
    incoming = lax.all_to_all(outgoing, "seq", split_axis=0, concat_axis=0, tiled=True)
    from_each = jnp.sum(
        (owner_core.reshape(n_cores, row_count) == core_index).astype(jnp.int32), axis=1
    )
    offsets = jnp.cumsum(from_each) - from_each
    target_rows = offsets[:, None] + row_ids[None, :]
    valid_rows = row_ids[None, :] < from_each[:, None]
    out_ids = jnp.arange(OWN_CAP, dtype=jnp.int32)
    placing = ((target_rows[None, :, :] == out_ids[:, None, None]) & valid_rows[None, :, :]).astype(
        jnp.bfloat16
    )
    return jnp.einsum("jsi,sic->jc", placing, incoming, preferred_element_type=jnp.float32).astype(
        jnp.bfloat16
    )


def solution(mesh):
    n_tensor = mesh.shape["tensor"]

    def step(tokens, gate_tiles, up_tiles, down_tiles, in_mask, out_mask, owner_core):
        form = on_device
        if grid_of(n_tensor)[1] == 2 and tokens.shape[1] % (2 * PIECES * gate_tiles.shape[1]) == 0:
            form = functools.partial(fused, n_tensor)
        return form(tokens, gate_tiles, up_tiles, down_tiles, in_mask, out_mask, owner_core)

    return jax.shard_map(
        step,
        mesh=mesh,
        in_specs=(
            P(("group", "seq"), "tensor"),
            P(("tensor", "seq"), None, None),
            P(("tensor", "seq"), None, None),
            P(("tensor", "seq"), None, None),
            P("tensor", None),
            P("tensor", None),
            P("group"),
        ),
        out_specs=P(("group", "seq"), "tensor"),
        check_vma=False,
    )
```
